32 devices in a mesh: wide: 16 (over z, y, x), deep: 2 (over core).
Axes of the slice: x: 2, y: 2, z: 4, core: 2. Of those that a mesh axis runs over, the one named last changes fastest.
Arguments:
- right_side: float32 [32, 128, 256], P('wide', 'deep'), may hold values from -12 to 12
- conductivity: float32 [32, 128, 256], P('wide', 'deep'), may hold values from 0.2 to 5
- checksum_weights: int32 [2, 16], replicated, may hold values from 1 to 15
- holder: int32 [16], replicated, may hold values from 0 to 15, as said below
Outputs:
- solution_field: float32 [32, 128, 256], P('wide', 'deep')
- residual: float32 [32, 128, 256], P('wide', 'deep')
- stored: float32 [32, 4, 4096], P('wide', None, 'deep')
The draws below stay inside these ranges and needn't reach their ends.
Inputs may be any that keep to these rules, and one draw needn't show every extreme that they name: No holder takes more than 2 pieces, and some take exactly 2; others take fewer or none.
All inputs are finite; a program needn't handle non-finite values.
Results may differ from the reference program's by a relative error of at most 0.00017.
Values sent between devices are 32-bit elements; how exact they have to be, the bound alone decides.
A program may use at most 64 MiB of HBM per device.

```python
import math
import jax
import jax.numpy as jnp
from jax import lax

CX = 2
CY = 64
CZ = 256
ITERS = 3
CHECKS = 2
HOLD = 2
NX = 32
NY = 128
NZ = 256
N_WIDE = 16
N_DEEP = 2


def draw_right_side(key, part):
    key = jax.random.fold_in(key, 11)
    position = jnp.arange(NX, dtype=jnp.float32)[:, None, None]
    ramp = 1.0 + 2.0 * position / (NX - 1)
    base = jnp.clip(jax.random.normal(key, (NX, NY, NZ), jnp.float32), -4.0, 4.0)
    return base * ramp


def draw_holder(key, part):
    key = jax.random.fold_in(key, 23)
    first_key, second_key = jax.random.split(key)
    ranks = jax.random.permutation(first_key, N_WIDE).astype(jnp.int32)
    devices = jax.random.permutation(second_key, N_WIDE).astype(jnp.int32)
    half = N_WIDE // 2
    group = jnp.where(ranks < half, ranks // HOLD, half // HOLD + (ranks - half))
    return devices[group].astype(jnp.int32)


def plant(entries, stream_key, least, top_value):
    extent = entries.shape
    index_at = [jax.random.randint(jax.random.fold_in(stream_key, axis), (), 0, extent[axis]) for axis in range(len(extent))]
    entries = entries.at[tuple(index_at)].set(least)
    longest = extent.index(max(extent))
    index_at[longest] = (index_at[longest] + 1) % extent[longest]
    return entries.at[tuple(index_at)].set(top_value)


def levels(own_key, dims, cuts, smallest, top_value):
    def one(dim, parts):
        steps = jax.random.uniform(jax.random.fold_in(jax.random.fold_in(own_key, 6), dim), (parts,), jnp.float32, smallest / len(cuts), top_value / len(cuts))
        return jnp.repeat(jnp.exp(steps), dims[dim] // parts).reshape((-1,) + (1,) * (len(dims) - dim - 1))

    factor_of = one(*cuts[0])
    for cut in cuts[1:]:
        factor_of = factor_of * one(*cut)
    return factor_of


def setup_inputs(seed: int = 0) -> dict:
    arg_keys = jax.random.split(jax.random.key(seed), 5)
    right_side = draw_right_side(jax.random.fold_in(arg_keys[4], 71), 0)
    conductivity = jnp.clip(jnp.exp(math.log(5.0) - 3.218876 * jax.random.uniform(arg_keys[1], (NX, NY, NZ), jnp.float32) ** levels(arg_keys[1], (NX, NY, NZ), ((0, 16), (1, 2)), -0.2, 0.2)), 0.2, 5.0)
    checksum_weights = plant(jax.random.randint(arg_keys[2], (CHECKS, N_WIDE), 1, 16), jax.random.fold_in(arg_keys[2], 1), 1, 15).astype(jnp.int32)
    holder = draw_holder(jax.random.fold_in(arg_keys[4], 71), 0)
    return dict(right_side=right_side, conductivity=conductivity, checksum_weights=checksum_weights, holder=holder)


OFFSETS = tuple(((a, b, c) for a in (-1, 0, 1) for b in (-1, 0, 1) for c in (-1, 0, 1) if (a, b, c) != (0, 0, 0)))

def coupling(offset):
    return (1.0, 0.5, 0.25)[abs(offset[0]) + abs(offset[1]) + abs(offset[2]) - 1]

def shifted(padded, offset):
    return padded[1 + offset[0]:1 + offset[0] + NX, 1 + offset[1]:1 + offset[1] + NY, 1 + offset[2]:1 + offset[2] + NZ]

def diagonal_of(conductivity, padded_conductivity):
    total = jnp.zeros_like(conductivity)
    for offset in OFFSETS:
        total = total + coupling(offset) * 0.5 * (conductivity + shifted(padded_conductivity, offset))
    return total

def operate(field, conductivity, padded_conductivity, diagonal):
    padded = jnp.pad(field, 1)
    total = diagonal * field
    for offset in OFFSETS:
        total = total - coupling(offset) * 0.5 * (conductivity + shifted(padded_conductivity, offset)) * shifted(padded, offset)
    return total

def checksums_of(field, weights_float, scales):
    blocks = field.reshape(N_WIDE, CX, NY, NZ)
    summed = jnp.einsum('kp,pxyz->kxyz', weights_float, blocks, precision=lax.Precision.HIGHEST)
    return summed * scales[:, None, None, None]

def reference(right_side, conductivity, checksum_weights, holder):
    padded_conductivity = jnp.pad(conductivity, 1)
    diagonal = diagonal_of(conductivity, padded_conductivity)
    solution_field = jnp.zeros_like(right_side)
    residual = right_side
    precond = residual / diagonal
    direction = precond
    product_now = jnp.sum(residual * precond)
    for iteration in range(ITERS):
        image = operate(direction, conductivity, padded_conductivity, diagonal)
        step_length = product_now / jnp.sum(direction * image)
        solution_field = solution_field + step_length * direction
        residual = residual - step_length * image
        precond = residual / diagonal
        product_next = jnp.sum(residual * precond)
        direction = precond + product_next / product_now * direction
        product_now = product_next
    weights_float = checksum_weights.astype(jnp.float32)
    scales = 1.0 / jnp.sqrt(lax.optimization_barrier(jnp.sum(weights_float * weights_float, axis=1)))
    checks = jnp.concatenate([checksums_of(solution_field, weights_float, scales), checksums_of(direction, weights_float, scales)], axis=0)
    piece_cells = CX * CY * CZ // N_WIDE
    rows_count = 2 * CHECKS
    blocks = checks.reshape(rows_count, CX, N_DEEP, CY, NZ).transpose(0, 2, 1, 3, 4)
    pieces = blocks.reshape(rows_count, N_DEEP, N_WIDE, piece_cells).transpose(2, 0, 1, 3)
    index_range = jnp.arange(N_WIDE, dtype=jnp.int32)
    same = holder[:, None] == holder[None, :]
    earlier = index_range[:, None] < index_range[None, :]
    slots = lax.optimization_barrier(jnp.sum((same & earlier).astype(jnp.int32), axis=0))
    targets = (holder * HOLD + slots).astype(jnp.int32)
    stored = jnp.zeros((N_WIDE * HOLD, rows_count, N_DEEP, piece_cells), jnp.float32).at[targets].set(pieces)
    stored = stored.reshape(N_WIDE * HOLD, rows_count, N_DEEP * piece_cells)
    return (solution_field, residual, stored)
```

```python
import functools

import jax
import jax.numpy as jnp
from jax import lax
from jax.experimental import pallas as pl
from jax.experimental.pallas import tpu as pltpu
from jax.sharding import PartitionSpec as P

ITERS = 3
HOLD = 2
PAD = 8
LANES = 128
SIDES = ((1, 0), (-1, 0), (0, 1), (0, -1), (1, 1), (1, -1), (-1, 1), (-1, -1))
MESH = pl.DeviceIdType.MESH


def span(step, source, count):
    if step == 0:
        return pl.ds(1, count)
    if source:
        return pl.ds(count if step > 0 else 1, 1)
    return pl.ds(0 if step > 0 else count + 1, 1)


def rows_of(step, source, count):
    if step == 0:
        return pl.ds(PAD, count)
    if source:
        return pl.ds(count if step > 0 else PAD, PAD)
    return pl.ds(0 if step > 0 else PAD + count, PAD)


def kernel(wide, deep, pieces, *refs):
    r_ref, k_ref, w_ref, h_ref = refs[:4]
    x_out, res_out, last_out = refs[4:7]
    (ext, zed, dirn, halo_send, halo_recv, pair, line, sum_send, sum_recv) = refs[7:16]
    planes, rows, cols = k_ref.shape
    w = lax.axis_index("wide")
    d = lax.axis_index("deep")

    def there(dx, dy):
        return (w + dx >= 0) & (w + dx < wide) & (d + dy >= 0) & (d + dy < deep)

    barrier = pltpu.get_barrier_semaphore()

    def greet_wide(i, carry):
        pl.semaphore_signal(barrier, inc=1, device_id=(lax.rem(w + i, wide), d), device_id_type=MESH)
        return carry

    def greet_deep(i, carry):
        pl.semaphore_signal(barrier, inc=1, device_id=(w, lax.rem(d + i, deep)), device_id_type=MESH)
        return carry

    lax.fori_loop(1, wide, greet_wide, 0)
    lax.fori_loop(1, deep, greet_deep, 0)
    greeted = jnp.int32(wide + deep - 2)
    for dx, dy in SIDES[4:]:
        there_now = there(dx, dy)
        greeted = greeted + jnp.where(there_now, 1, 0)

        @pl.when(there_now)
        def _():
            pl.semaphore_signal(barrier, inc=1, device_id=(w + dx, d + dy), device_id_type=MESH)

    for phase in range(4):
        for dx, dy in SIDES:

            @pl.when(jnp.logical_not(there(-dx, -dy)))
            def _():
                at = (phase, span(dx, False, planes), rows_of(dy, False, rows))
                ext[at] = jnp.zeros_like(ext[at])

    inner = (slice(1, planes + 1), slice(PAD, PAD + rows))
    ext[(0,) + inner] = k_ref[...]

    if pieces:
        (field, parts, landed, sums, chosen, choose, final, all_send, all_recv) = refs[16:]
        lane = lax.broadcasted_iota(jnp.int32, (1, 4 * wide), 1)
        place = jnp.zeros((1, 4 * wide), jnp.int32)
        hold = [h_ref[j] for j in range(wide)]
        for j in range(wide):
            slot = jnp.int32(0)
            for i in range(j):
                slot = slot + jnp.where(hold[i] == hold[j], 1, 0)
            place = jnp.where(lane % wide == j, hold[j] * HOLD + slot, place)
        line_no = lax.broadcasted_iota(jnp.int32, (8 * wide, 4 * wide), 0)
        lane_no = lax.broadcasted_iota(jnp.int32, (8 * wide, 4 * wide), 1)
        hit = (line_no // 4 == place) & (line_no % 4 == lane_no // wide)
        choose[...] = jnp.where(hit, 1.0, 0.0).astype(jnp.float32)

    def halo_copy(phase, side):
        dx, dy = SIDES[side]
        return pltpu.make_async_remote_copy(
            src_ref=ext.at[phase, span(dx, True, planes), rows_of(dy, True, rows)],
            dst_ref=ext.at[phase, span(dx, False, planes), rows_of(dy, False, rows)],
            send_sem=halo_send.at[phase, side],
            recv_sem=halo_recv.at[phase, side],
            device_id=(w + dx, d + dy),
            device_id_type=MESH,
        )

    def halo_start(phase):
        for side, (dx, dy) in enumerate(SIDES):

            @pl.when(there(dx, dy))
            def _():
                halo_copy(phase, side).start()

    def halo_wait(phase):
        for side, (dx, dy) in enumerate(SIDES):

            @pl.when(there(-dx, -dy))
            def _():
                halo_copy(phase, side).wait_recv()

    def halo_sent(phase):
        for side, (dx, dy) in enumerate(SIDES):

            @pl.when(there(dx, dy))
            def _():
                halo_copy(phase, side).wait_send()

    col = lax.broadcasted_iota(jnp.int32, (rows, cols), 1)

    def smooth(block):
        result = []
        for x in range(planes):
            t = 0.5 * (block[x] + block[x + 2]) + block[x + 1]
            tall = t.shape[0]
            t = 0.5 * (pltpu.roll(t, 1, 0) + pltpu.roll(t, tall - 1, 0)) + t
            t = t[PAD:PAD + rows]
            left = jnp.where(col == 0, 0.0, pltpu.roll(t, 1, 1))
            right = jnp.where(col == cols - 1, 0.0, pltpu.roll(t, cols - 1, 1))
            result.append(0.5 * (left + right) + t)
        return result

    pl.semaphore_wait(barrier, greeted)
    halo_start(0)
    halo_wait(0)

    kappa = [ext[0, x] for x in range(planes + 2)]
    blurred = smooth(kappa)
    mine = [k_ref[x] for x in range(planes)]
    diagonal = [6.0 * mine[x] + blurred[x] for x in range(planes)]
    inverse = [1.0 / diagonal[x] for x in range(planes)]
    for x in range(planes):
        ext[1, x + 1, PAD:PAD + rows] = r_ref[x] * inverse[x]
    halo_start(1)
    halo_wait(1)

    lane1 = lax.broadcasted_iota(jnp.int32, (1, LANES), 1)

    def total_of(turn, values):
        row = jnp.zeros((1, LANES), jnp.float32)
        for i, value in enumerate(values):
            one = value[0]
            for x in range(1, planes):
                one = one + value[x]
            one = jnp.sum(jnp.sum(one, axis=0, keepdims=True), axis=1, keepdims=True)
            row = jnp.where(lane1 == i, one, row)
        pair[turn, d] = row

        def to_deep(i, carry):
            pltpu.make_async_remote_copy(
                src_ref=pair.at[turn, d], dst_ref=pair.at[turn, d],
                send_sem=sum_send.at[turn, 0], recv_sem=sum_recv.at[turn, 0],
                device_id=(w, lax.rem(d + i, deep)), device_id_type=MESH,
            ).start()
            return carry

        lax.fori_loop(1, deep, to_deep, 0)
        some = pair.at[turn, pl.ds(0, deep - 1)]
        pltpu.make_async_copy(some, some, sum_recv.at[turn, 0]).wait()
        row = pair[turn, 0]
        for i in range(1, deep):
            row = row + pair[turn, i]
        line[turn, w] = row

        def to_wide(i, carry):
            pltpu.make_async_remote_copy(
                src_ref=line.at[turn, w], dst_ref=line.at[turn, w],
                send_sem=sum_send.at[turn, 1], recv_sem=sum_recv.at[turn, 1],
                device_id=(lax.rem(w + i, wide), d), device_id_type=MESH,
            ).start()
            return carry

        lax.fori_loop(1, wide, to_wide, 0)
        some = line.at[turn, pl.ds(0, wide - 1)]
        pltpu.make_async_copy(some, some, sum_recv.at[turn, 1]).wait()
        row = jnp.sum(line[turn], axis=0)
        return [row[:, i:i + 1] for i in range(len(values))]

    for turn in range(ITERS):
        before = 1 if turn == 0 else None
        block = [ext[1, x] if before else dirn[x] for x in range(planes + 2)]
        own = [block[x + 1][PAD:PAD + rows] for x in range(planes)]
        first = smooth(block)
        second = smooth([ext[0, x] * block[x] for x in range(planes + 2)])
        image, spread = [], []
        for x in range(planes):
            k = k_ref[x]
            image.append((diagonal[x] + 2.0 * k) * own[x] - k * first[x] - second[x])
            spread.append(image[x] * inverse[x])
        carries_on = turn < ITERS - 1
        if carries_on:
            for x in range(planes):
                ext[turn + 2, x + 1, PAD:PAD + rows] = spread[x]
            halo_start(turn + 2)
        rest = [r_ref[x] if turn == 0 else res_out[x] for x in range(planes)]
        if turn == 0:
            near = own
        else:
            near = [zed[x + 1, PAD:PAD + rows] for x in range(planes)]
        both = range(planes)
        rz, pq, zq, qq = total_of(turn, [
            [rest[x] * near[x] for x in both],
            [own[x] * image[x] for x in both],
            [rest[x] * spread[x] for x in both],
            [image[x] * spread[x] for x in both],
        ])
        step = rz / pq
        later = rz - 2.0 * step * zq + step * step * qq
        ratio = later / rz
        for x in both:
            base = step * own[x]
            x_out[x] = base if turn == 0 else x_out[x] + base
            res_out[x] = rest[x] - step * image[x]
        if carries_on:
            halo_wait(turn + 2)
            for x in range(planes + 2):
                old = ext[1, x] if turn == 0 else zed[x]
                new = old - step * ext[turn + 2, x]
                zed[x] = new
                dirn[x] = new + ratio * block[x]
        else:
            final_dirn = [near[x] - step * spread[x] + ratio * own[x] for x in both]

    if pieces:
        halves = cols // LANES
        for f in range(2):
            for x in range(planes):
                value = x_out[x] if f == 0 else final_dirn[x]
                for s in range(halves):
                    field[f, s, x * rows:(x + 1) * rows] = value[:, s * LANES:(s + 1) * LANES]
        stride = planes * rows // wide
        for c in range(wide):
            for f in range(2):
                parts[c, f * wide:(f + 1) * wide] = field[
                    f, c % halves, pl.ds(c // halves, wide, stride=stride), :]
        landed[w] = parts[w]

        def scatter(i, carry):
            q = lax.rem(w + i, wide)
            pltpu.make_async_remote_copy(
                src_ref=parts.at[q], dst_ref=landed.at[w],
                send_sem=all_send.at[0], recv_sem=all_recv.at[0],
                device_id=(q, d), device_id_type=MESH,
            ).start()
            return carry

        lax.fori_loop(1, wide, scatter, 0)
        some = landed.at[pl.ds(0, wide - 1)]
        pltpu.make_async_copy(some, some, all_recv.at[0]).wait()
        for k in range(2):
            squares = jnp.int32(0)
            for p in range(wide):
                squares = squares + w_ref[k, p] * w_ref[k, p]
            scale = 1.0 / jnp.sqrt(jnp.full((1, LANES), squares.astype(jnp.float32)))
            for f in range(2):
                total = jnp.zeros((wide, LANES), jnp.float32)
                for p in range(wide):
                    total = total + w_ref[k, p].astype(jnp.float32) * landed[p, f * wide:(f + 1) * wide]
                at = (2 * f + k) * wide
                sums[at:at + wide] = total * scale
        chosen[...] = jnp.dot(
            choose[...], sums[...], precision=lax.Precision.HIGHEST,
            preferred_element_type=jnp.float32)

        def slot_rows(q):
            return pl.ds(pl.multiple_of(q * 8, 8), 8)

        here = pl.ds(pl.multiple_of(w * LANES, LANES), LANES)
        final[:, here] = chosen[slot_rows(w), :]

        def deliver(i, carry):
            q = lax.rem(w + i, wide)
            pltpu.make_async_remote_copy(
                src_ref=chosen.at[slot_rows(q)], dst_ref=final.at[:, here],
                send_sem=all_send.at[1], recv_sem=all_recv.at[1],
                device_id=(q, d), device_id_type=MESH,
            ).start()
            return carry

        lax.fori_loop(1, wide, deliver, 0)
        some = final.at[:, pl.ds(0, (wide - 1) * LANES)]
        pltpu.make_async_copy(some, some, all_recv.at[1]).wait()
        last_out[...] = final[...]
        some = parts.at[pl.ds(0, wide - 1)]
        pltpu.make_async_copy(some, some, all_send.at[0]).wait()
        some = chosen.at[pl.ds(0, (wide - 1) * 8)]
        pltpu.make_async_copy(some, some, all_send.at[1]).wait()
    else:
        for x in range(planes):
            last_out[x] = final_dirn[x]

    for phase in range(4):
        halo_sent(phase)
    for turn in range(ITERS):
        some = pair.at[turn, pl.ds(0, deep - 1)]
        pltpu.make_async_copy(some, some, sum_send.at[turn, 0]).wait()
        some = line.at[turn, pl.ds(0, wide - 1)]
        pltpu.make_async_copy(some, some, sum_send.at[turn, 1]).wait()


def store_pieces(solution_field, direction, checksum_weights, holder):
    width = lax.axis_size("wide")
    position = lax.axis_index("wide")
    weights_float = checksum_weights.astype(jnp.float32)
    scales = 1.0 / jnp.sqrt(jnp.sum(weights_float * weights_float, axis=1))
    scaled_weights = weights_float * scales[:, None]
    checks_count = checksum_weights.shape[0]
    flat = jnp.stack([solution_field, direction]).reshape(2, -1)
    cells = flat.shape[1]
    mine = lax.dynamic_slice_in_dim(scaled_weights, position, 1, 1)[:, 0]
    terms = (flat[:, None, :] * mine[None, :, None]).reshape(2 * checks_count, cells)
    piece = lax.psum_scatter(terms, "wide", scatter_dimension=1, tiled=True)
    index_range = jnp.arange(width, dtype=jnp.int32)
    same = holder[:, None] == holder[None, :]
    earlier = index_range[:, None] < index_range[None, :]
    slots = jnp.sum((same & earlier).astype(jnp.int32), axis=0)
    slot_range = jnp.arange(HOLD, dtype=jnp.int32)
    select = ((holder[None, :] == position) & (slots[None, :] == slot_range[:, None])).astype(
        jnp.float32
    )
    target = (index_range == holder[position]).astype(jnp.float32)
    outgoing = target[:, None, None] * piece[None, :, :]
    arrived = lax.all_to_all(outgoing, "wide", split_axis=0, concat_axis=0, tiled=True)
    return jnp.einsum("sj,jfc->sfc", select, arrived, precision=lax.Precision.HIGHEST)


def body(right_side, conductivity, checksum_weights, holder):
    wide, deep = lax.axis_size("wide"), lax.axis_size("deep")
    planes, rows, cols = conductivity.shape
    cells = planes * rows * cols
    pieces = cells == wide * wide * LANES and checksum_weights.shape[0] == 2 and HOLD == 2
    block = jax.ShapeDtypeStruct(conductivity.shape, jnp.float32)
    vmem = pl.BlockSpec(memory_space=pltpu.VMEM)
    smem = pl.BlockSpec(memory_space=pltpu.SMEM)
    tall = (planes + 2, rows + 2 * PAD, cols)
    scratch = [
        pltpu.VMEM((4,) + tall, jnp.float32),
        pltpu.VMEM(tall, jnp.float32),
        pltpu.VMEM(tall, jnp.float32),
        pltpu.SemaphoreType.DMA((4, 8)),
        pltpu.SemaphoreType.DMA((4, 8)),
        pltpu.VMEM((ITERS, deep, 1, LANES), jnp.float32),
        pltpu.VMEM((ITERS, wide, 1, LANES), jnp.float32),
        pltpu.SemaphoreType.DMA((ITERS, 2)),
        pltpu.SemaphoreType.DMA((ITERS, 2)),
    ]
    last = block
    if pieces:
        last = jax.ShapeDtypeStruct((8, wide * LANES), jnp.float32)
        scratch += [
            pltpu.VMEM((2, cols // LANES, planes * rows, LANES), jnp.float32),
            pltpu.VMEM((wide, 2 * wide, LANES), jnp.float32),
            pltpu.VMEM((wide, 2 * wide, LANES), jnp.float32),
            pltpu.VMEM((4 * wide, LANES), jnp.float32),
            pltpu.VMEM((8 * wide, LANES), jnp.float32),
            pltpu.VMEM((8 * wide, 4 * wide), jnp.float32),
            pltpu.VMEM((8, wide * LANES), jnp.float32),
            pltpu.SemaphoreType.DMA((2,)),
            pltpu.SemaphoreType.DMA((2,)),
        ]
    solution_field, residual, rest = pl.pallas_call(
        functools.partial(kernel, wide, deep, pieces),
        out_shape=[block, block, last],
        in_specs=[vmem, vmem, smem, smem],
        out_specs=[vmem, vmem, vmem],
        scratch_shapes=scratch,
        compiler_params=pltpu.CompilerParams(
            collective_id=0, has_side_effects=True, vmem_limit_bytes=32 * 1024 * 1024
        ),
    )(right_side, conductivity, checksum_weights, holder)
    if pieces:
        stored = rest.reshape(HOLD, 4, wide * LANES)
    else:
        stored = store_pieces(solution_field, rest, checksum_weights, holder)
    return (solution_field, residual, stored)


def solution(mesh):
    placed = (P("wide", "deep", None), P("wide", "deep", None), P(), P())
    return jax.shard_map(
        body,
        mesh=mesh,
        in_specs=placed,
        out_specs=(P("wide", "deep", None), P("wide", "deep", None), P("wide", None, "deep")),
        check_vma=False,
    )
```

```python
import functools

import jax
import jax.numpy as jnp
from jax import lax
from jax.experimental import pallas as pl
from jax.experimental.pallas import tpu as pltpu
from jax.sharding import PartitionSpec as P

ITERS = 3
HOLD = 2
PAD = 8
LANES = 128
SIDES = ((1, 0), (-1, 0), (0, 1), (0, -1), (1, 1), (1, -1), (-1, 1), (-1, -1))
MESH = pl.DeviceIdType.MESH


def span(step, source, count):
    if step == 0:
        return pl.ds(1, count)
    if source:
        return pl.ds(count if step > 0 else 1, 1)
    return pl.ds(0 if step > 0 else count + 1, 1)


def rows_of(step, source, count):
    if step == 0:
        return pl.ds(PAD, count)
    if source:
        return pl.ds(count if step > 0 else PAD, PAD)
    return pl.ds(0 if step > 0 else PAD + count, PAD)


def kernel(wide, deep, pieces, *refs):
    r_in, k_in, w_in, h_in = refs[:4]
    x_out, res_out, last_out = refs[4:7]
    (ext, zed, dirn, halo_send, halo_recv, pair, line, sum_send, sum_recv) = refs[7:16]
    r_ref, w_ref, h_ref, load_sem = refs[16:20]
    planes, rows, cols = r_ref.shape
    inner = (pl.ds(1, planes), pl.ds(PAD, rows))
    loads = [
        pltpu.make_async_copy(k_in, ext.at[(0,) + inner], load_sem.at[0]),
        pltpu.make_async_copy(r_in, r_ref, load_sem.at[1]),
        pltpu.make_async_copy(w_in, w_ref, load_sem.at[2]),
        pltpu.make_async_copy(h_in, h_ref, load_sem.at[3]),
    ]
    for load in loads:
        load.start()
    w = lax.axis_index("wide")
    d = lax.axis_index("deep")

    def there(dx, dy):
        return (w + dx >= 0) & (w + dx < wide) & (d + dy >= 0) & (d + dy < deep)

    barrier = pltpu.get_barrier_semaphore()

    def greet_wide(i, carry):
        pl.semaphore_signal(barrier, inc=1, device_id=(lax.rem(w + i, wide), d), device_id_type=MESH)
        return carry

    def greet_deep(i, carry):
        pl.semaphore_signal(barrier, inc=1, device_id=(w, lax.rem(d + i, deep)), device_id_type=MESH)
        return carry

    lax.fori_loop(1, wide, greet_wide, 0)
    lax.fori_loop(1, deep, greet_deep, 0)
    greeted = jnp.int32(wide + deep - 2)
    for dx, dy in SIDES[4:]:
        there_now = there(dx, dy)
        greeted = greeted + jnp.where(there_now, 1, 0)

        @pl.when(there_now)
        def _():
            pl.semaphore_signal(barrier, inc=1, device_id=(w + dx, d + dy), device_id_type=MESH)

    def halo_copy(phase, side):
        dx, dy = SIDES[side]
        return pltpu.make_async_remote_copy(
            src_ref=ext.at[phase, span(dx, True, planes), rows_of(dy, True, rows)],
            dst_ref=ext.at[phase, span(dx, False, planes), rows_of(dy, False, rows)],
            send_sem=halo_send.at[phase, side],
            recv_sem=halo_recv.at[phase, side],
            device_id=(w + dx, d + dy),
            device_id_type=MESH,
        )

    def halo_start(phase):
        for side, (dx, dy) in enumerate(SIDES):

            @pl.when(there(dx, dy))
            def _():
                halo_copy(phase, side).start()

    def halo_wait(phase):
        for side, (dx, dy) in enumerate(SIDES):

            @pl.when(there(-dx, -dy))
            def _():
                halo_copy(phase, side).wait_recv()

    def halo_sent(phase):
        for side, (dx, dy) in enumerate(SIDES):

            @pl.when(there(dx, dy))
            def _():
                halo_copy(phase, side).wait_send()

    col = lax.broadcasted_iota(jnp.int32, (rows, cols), 1)

    def smooth(block):
        result = []
        for x in range(planes):
            t = 0.5 * (block[x] + block[x + 2]) + block[x + 1]
            tall = t.shape[0]
            t = 0.5 * (pltpu.roll(t, 1, 0) + pltpu.roll(t, tall - 1, 0)) + t
            t = t[PAD:PAD + rows]
            left = jnp.where(col == 0, 0.0, pltpu.roll(t, 1, 1))
            right = jnp.where(col == cols - 1, 0.0, pltpu.roll(t, cols - 1, 1))
            result.append(0.5 * (left + right) + t)
        return result

    def clear(phase):
        for dx, dy in SIDES:

            @pl.when(jnp.logical_not(there(-dx, -dy)))
            def _():
                at = (phase, span(dx, False, planes), rows_of(dy, False, rows))
                ext[at] = jnp.zeros_like(ext[at])

    loads[0].wait()
    pl.semaphore_wait(barrier, greeted)
    halo_start(0)
    for phase in range(4):
        clear(phase)
    for load in loads[1:]:
        load.wait()
    if pieces:
        (field, parts, landed, sums, weigh, chosen, choose, final, all_send, all_recv) = refs[20:]
        lane = lax.broadcasted_iota(jnp.int32, (1, 4 * wide), 1)
        place = jnp.zeros((1, 4 * wide), jnp.int32)
        hold = [h_ref[j] for j in range(wide)]
        for j in range(wide):
            slot = jnp.int32(0)
            for i in range(j):
                slot = slot + jnp.where(hold[i] == hold[j], 1, 0)
            place = jnp.where(lane % wide == j, hold[j] * HOLD + slot, place)
        line_no = lax.broadcasted_iota(jnp.int32, (8 * wide, 4 * wide), 0)
        lane_no = lax.broadcasted_iota(jnp.int32, (8 * wide, 4 * wide), 1)
        hit = (line_no // 4 == place) & (line_no % 4 == lane_no // wide)
        choose[...] = jnp.where(hit, 1.0, 0.0).astype(jnp.float32)
        for k in range(2):
            squares = jnp.int32(0)
            for p in range(wide):
                squares = squares + w_ref[k, p] * w_ref[k, p]
            scale = 1.0 / jnp.sqrt(jnp.full((1, LANES), squares, jnp.int32).astype(jnp.float32))
            for p in range(wide):
                whole = jnp.full((1, LANES), w_ref[k, p], jnp.int32).astype(jnp.float32)
                weigh[k, p:p + 1] = whole * scale

    halo_wait(0)

    kappa = [ext[0, x] for x in range(planes + 2)]
    blurred = smooth(kappa)
    mine = [kappa[x + 1][PAD:PAD + rows] for x in range(planes)]
    diagonal = [6.0 * mine[x] + blurred[x] for x in range(planes)]
    inverse = [1.0 / diagonal[x] for x in range(planes)]
    for x in range(planes):
        ext[1, x + 1, PAD:PAD + rows] = r_ref[x] * inverse[x]
    halo_start(1)
    halo_wait(1)

    lane1 = lax.broadcasted_iota(jnp.int32, (1, LANES), 1)

    def total_of(turn, values):
        row = jnp.zeros((1, LANES), jnp.float32)
        for i, value in enumerate(values):
            one = value[0]
            for x in range(1, planes):
                one = one + value[x]
            one = jnp.sum(jnp.sum(one, axis=0, keepdims=True), axis=1, keepdims=True)
            row = jnp.where(lane1 == i, one, row)
        pair[turn, d] = row

        def to_deep(i, carry):
            pltpu.make_async_remote_copy(
                src_ref=pair.at[turn, d], dst_ref=pair.at[turn, d],
                send_sem=sum_send.at[turn, 0], recv_sem=sum_recv.at[turn, 0],
                device_id=(w, lax.rem(d + i, deep)), device_id_type=MESH,
            ).start()
            return carry

        lax.fori_loop(1, deep, to_deep, 0)
        some = pair.at[turn, pl.ds(0, deep - 1)]
        pltpu.make_async_copy(some, some, sum_recv.at[turn, 0]).wait()
        row = pair[turn, 0]
        for i in range(1, deep):
            row = row + pair[turn, i]
        line[turn, w] = row

        def to_wide(i, carry):
            pltpu.make_async_remote_copy(
                src_ref=line.at[turn, w], dst_ref=line.at[turn, w],
                send_sem=sum_send.at[turn, 1], recv_sem=sum_recv.at[turn, 1],
                device_id=(lax.rem(w + i, wide), d), device_id_type=MESH,
            ).start()
            return carry

        lax.fori_loop(1, wide, to_wide, 0)
        some = line.at[turn, pl.ds(0, wide - 1)]
        pltpu.make_async_copy(some, some, sum_recv.at[turn, 1]).wait()
        row = jnp.sum(line[turn], axis=0)
        return [row[:, i:i + 1] for i in range(len(values))]

    for turn in range(ITERS):
        before = 1 if turn == 0 else None
        block = [ext[1, x] if before else dirn[x] for x in range(planes + 2)]
        own = [block[x + 1][PAD:PAD + rows] for x in range(planes)]
        first = smooth(block)
        second = smooth([ext[0, x] * block[x] for x in range(planes + 2)])
        image, spread = [], []
        for x in range(planes):
            k = ext[0, x + 1, PAD:PAD + rows]
            image.append((diagonal[x] + 2.0 * k) * own[x] - k * first[x] - second[x])
            spread.append(image[x] * inverse[x])
        carries_on = turn < ITERS - 1
        if carries_on:
            for x in range(planes):
                ext[turn + 2, x + 1, PAD:PAD + rows] = spread[x]
            halo_start(turn + 2)
        rest = [r_ref[x] if turn == 0 else res_out[x] for x in range(planes)]
        if turn == 0:
            near = own
        else:
            near = [zed[x + 1, PAD:PAD + rows] for x in range(planes)]
        both = range(planes)
        rz, pq, zq, qq = total_of(turn, [
            [rest[x] * near[x] for x in both],
            [own[x] * image[x] for x in both],
            [rest[x] * spread[x] for x in both],
            [image[x] * spread[x] for x in both],
        ])
        step = rz / pq
        later = rz - 2.0 * step * zq + step * step * qq
        ratio = later / rz
        for x in both:
            base = step * own[x]
            x_out[x] = base if turn == 0 else x_out[x] + base
            res_out[x] = rest[x] - step * image[x]
        if carries_on:
            halo_wait(turn + 2)
            for x in range(planes + 2):
                old = ext[1, x] if turn == 0 else zed[x]
                new = old - step * ext[turn + 2, x]
                zed[x] = new
                dirn[x] = new + ratio * block[x]
        else:
            final_dirn = [near[x] - step * spread[x] + ratio * own[x] for x in both]

    if pieces:
        halves = cols // LANES
        for f in range(2):
            for x in range(planes):
                value = x_out[x] if f == 0 else final_dirn[x]
                for s in range(halves):
                    field[f, s, x * rows:(x + 1) * rows] = value[:, s * LANES:(s + 1) * LANES]
        stride = planes * rows // wide
        for c in range(wide):
            for f in range(2):
                parts[c, f * wide:(f + 1) * wide] = field[
                    f, c % halves, pl.ds(c // halves, wide, stride=stride), :]
        landed[w] = parts[w]

        def scatter(q):
            return pltpu.make_async_remote_copy(
                src_ref=parts.at[q], dst_ref=landed.at[w],
                send_sem=all_send.at[0], recv_sem=all_recv.at[0],
                device_id=(q, d), device_id_type=MESH,
            )

        for i in range(1, wide):
            scatter(jnp.bitwise_xor(w, i)).start()
        some = landed.at[pl.ds(0, wide - 1)]
        pltpu.make_async_copy(some, some, all_recv.at[0]).wait()
        for k in range(2):
            for f in range(2):
                total = jnp.zeros((wide, LANES), jnp.float32)
                for p in range(wide):
                    total = total + weigh[k, p:p + 1] * landed[p, f * wide:(f + 1) * wide]
                at = (2 * f + k) * wide
                sums[at:at + wide] = total
        chosen[...] = jnp.dot(
            choose[...], sums[...], precision=lax.Precision.HIGHEST,
            preferred_element_type=jnp.float32)

        def slot_rows(q):
            return pl.ds(pl.multiple_of(q * 8, 8), 8)

        here = pl.ds(pl.multiple_of(w * LANES, LANES), LANES)
        final[:, here] = chosen[slot_rows(w), :]

        def deliver(i, carry):
            q = lax.rem(w + i, wide)
            pltpu.make_async_remote_copy(
                src_ref=chosen.at[slot_rows(q)], dst_ref=final.at[:, here],
                send_sem=all_send.at[1], recv_sem=all_recv.at[1],
                device_id=(q, d), device_id_type=MESH,
            ).start()
            return carry

        lax.fori_loop(1, wide, deliver, 0)
        some = final.at[:, pl.ds(0, (wide - 1) * LANES)]
        pltpu.make_async_copy(some, some, all_recv.at[1]).wait()
        last_out[0] = final[0:4]
        last_out[1] = final[4:8]
        some = parts.at[pl.ds(0, wide - 1)]
        pltpu.make_async_copy(some, some, all_send.at[0]).wait()
        some = chosen.at[pl.ds(0, (wide - 1) * 8)]
        pltpu.make_async_copy(some, some, all_send.at[1]).wait()
    else:
        for x in range(planes):
            last_out[x] = final_dirn[x]

    for phase in range(4):
        halo_sent(phase)
    for turn in range(ITERS):
        some = pair.at[turn, pl.ds(0, deep - 1)]
        pltpu.make_async_copy(some, some, sum_send.at[turn, 0]).wait()
        some = line.at[turn, pl.ds(0, wide - 1)]
        pltpu.make_async_copy(some, some, sum_send.at[turn, 1]).wait()


def store_pieces(solution_field, direction, checksum_weights, holder):
    width = lax.axis_size("wide")
    position = lax.axis_index("wide")
    weights_float = checksum_weights.astype(jnp.float32)
    scales = 1.0 / jnp.sqrt(jnp.sum(weights_float * weights_float, axis=1))
    scaled_weights = weights_float * scales[:, None]
    checks_count = checksum_weights.shape[0]
    flat = jnp.stack([solution_field, direction]).reshape(2, -1)
    cells = flat.shape[1]
    mine = lax.dynamic_slice_in_dim(scaled_weights, position, 1, 1)[:, 0]
    terms = (flat[:, None, :] * mine[None, :, None]).reshape(2 * checks_count, cells)
    piece = lax.psum_scatter(terms, "wide", scatter_dimension=1, tiled=True)
    index_range = jnp.arange(width, dtype=jnp.int32)
    same = holder[:, None] == holder[None, :]
    earlier = index_range[:, None] < index_range[None, :]
    slots = jnp.sum((same & earlier).astype(jnp.int32), axis=0)
    slot_range = jnp.arange(HOLD, dtype=jnp.int32)
    select = ((holder[None, :] == position) & (slots[None, :] == slot_range[:, None])).astype(
        jnp.float32
    )
    target = (index_range == holder[position]).astype(jnp.float32)
    outgoing = target[:, None, None] * piece[None, :, :]
    arrived = lax.all_to_all(outgoing, "wide", split_axis=0, concat_axis=0, tiled=True)
    return jnp.einsum("sj,jfc->sfc", select, arrived, precision=lax.Precision.HIGHEST)


def body(right_side, conductivity, checksum_weights, holder):
    wide, deep = lax.axis_size("wide"), lax.axis_size("deep")
    planes, rows, cols = conductivity.shape
    cells = planes * rows * cols
    pieces = cells == wide * wide * LANES and wide & (wide - 1) == 0 and checksum_weights.shape[0] == 2 and HOLD == 2
    block = jax.ShapeDtypeStruct(conductivity.shape, jnp.float32)
    vmem = pl.BlockSpec(memory_space=pltpu.VMEM)
    anywhere = pl.BlockSpec(memory_space=pltpu.HBM)
    tall = (planes + 2, rows + 2 * PAD, cols)
    scratch = [
        pltpu.VMEM((4,) + tall, jnp.float32),
        pltpu.VMEM(tall, jnp.float32),
        pltpu.VMEM(tall, jnp.float32),
        pltpu.SemaphoreType.DMA((4, 8)),
        pltpu.SemaphoreType.DMA((4, 8)),
        pltpu.VMEM((ITERS, deep, 1, LANES), jnp.float32),
        pltpu.VMEM((ITERS, wide, 1, LANES), jnp.float32),
        pltpu.SemaphoreType.DMA((ITERS, 2)),
        pltpu.SemaphoreType.DMA((ITERS, 2)),
        pltpu.VMEM(conductivity.shape, jnp.float32),
        pltpu.SMEM(checksum_weights.shape, jnp.int32),
        pltpu.SMEM(holder.shape, jnp.int32),
        pltpu.SemaphoreType.DMA((4,)),
    ]
    last = block
    if pieces:
        last = jax.ShapeDtypeStruct((HOLD, 4, wide * LANES), jnp.float32)
        scratch += [
            pltpu.VMEM((2, cols // LANES, planes * rows, LANES), jnp.float32),
            pltpu.VMEM((wide, 2 * wide, LANES), jnp.float32),
            pltpu.VMEM((wide, 2 * wide, LANES), jnp.float32),
            pltpu.VMEM((4 * wide, LANES), jnp.float32),
            pltpu.VMEM((2, wide, LANES), jnp.float32),
            pltpu.VMEM((8 * wide, LANES), jnp.float32),
            pltpu.VMEM((8 * wide, 4 * wide), jnp.float32),
            pltpu.VMEM((8, wide * LANES), jnp.float32),
            pltpu.SemaphoreType.DMA((2,)),
            pltpu.SemaphoreType.DMA((2,)),
        ]
    arguments = [
        pltpu.with_memory_space_constraint(a, pltpu.HBM)
        for a in (right_side, conductivity, checksum_weights, holder)
    ]
    solution_field, residual, rest = pl.pallas_call(
        functools.partial(kernel, wide, deep, pieces),
        out_shape=[block, block, last],
        in_specs=[anywhere] * 4,
        out_specs=[vmem, vmem, vmem],
        scratch_shapes=scratch,
        compiler_params=pltpu.CompilerParams(
            collective_id=0, has_side_effects=True, vmem_limit_bytes=24 * 1024 * 1024
        ),
    )(*arguments)
    if pieces:
        stored = rest
    else:
        stored = store_pieces(solution_field, rest, checksum_weights, holder)
    return (solution_field, residual, stored)


def solution(mesh):
    placed = (P("wide", "deep", None), P("wide", "deep", None), P(), P())
    return jax.shard_map(
        body,
        mesh=mesh,
        in_specs=placed,
        out_specs=(P("wide", "deep", None), P("wide", "deep", None), P("wide", None, "deep")),
        check_vma=False,
    )
```
